256 devices in a mesh: blk: 8 (over x_lo, y), uly: 32 (over x_hi, z, core).
Axes of the slice: x: 4 (x_hi: 2, x_lo: 2; x = x_hi * 2 + x_lo), y: 4, z: 8, core: 2. Of those that a mesh axis runs over, the one named last changes fastest.
Arguments:
- queries: bfloat16 [32768, 4096], P(('blk', 'uly')), may hold values from -8 to 8
- keys: bfloat16 [32768, 4096], P(('blk', 'uly')), may hold values from -8 to 8
- values: bfloat16 [32768, 4096], P(('blk', 'uly')), may hold values from -6 to 6
- grad_out: bfloat16 [32768, 4096], P(('blk', 'uly')), may hold values from -6 to 6
- doc_start: int32 [256], replicated, may hold values from 0 to 32640, as said below
Outputs:
- grad_queries: bfloat16 [32768, 4096], P(('blk', 'uly'))
- grad_keys: bfloat16 [32768, 4096], P(('blk', 'uly'))
- grad_values: bfloat16 [32768, 4096], P(('blk', 'uly'))
The draws below stay inside these ranges and needn't reach their ends.
Inputs may be any that keep to these rules, and one draw needn't show every extreme that they name: `doc_start`: each entry is the first position of its block's document, so documents are runs of whole blocks; no document is longer than 8 blocks and one is exactly 8; a document crosses every boundary between groups of 4096 positions and starts at most 7 blocks before it, at one boundary exactly 7; the last block starts a document.
All inputs are finite; a program needn't handle non-finite values.
Results may differ from the reference program's by a relative error of at most 0.0051.
Values may be sent and summed in bfloat16 or wider, within the bound.
No kernel may reach another device: no remote copies, remote signals or barrier semaphores. Data moves between devices by JAX's collectives and lax.ppermute only.
A program may use at most 64 MiB of HBM per device.

```python
import math
from functools import partial
import jax
import jax.numpy as jnp
from jax import lax

HD = 128
ROWS = 128
BLOCK = 128
MAXB = 8
HEADS = 32
SEQ = 32768
NBLOCKS = 256
N_BLK = 8
N_ULY = 32


def base_draw(key):
    return jnp.clip(jax.random.normal(key, (SEQ, HEADS * HD), jnp.float32), -4.0, 4.0)


def draw_queries(key, part):
    base = base_draw(jax.random.fold_in(key, 1))
    return base.astype(jnp.bfloat16)


def draw_keys(key, part):
    base = base_draw(jax.random.fold_in(key, 2))
    return base.astype(jnp.bfloat16)


def draw_doc_start(key, part):
    group_blocks = N_ULY * ROWS // BLOCK
    bounds = N_BLK - 1
    key_reach, key_before, key_extra, key_flags = jax.random.split(key, 4)
    reach = jax.random.randint(key_reach, (), 0, bounds)
    which = jnp.arange(bounds)
    before = jax.random.randint(key_before, (bounds,), 1, MAXB)
    before = jnp.where(which == reach, MAXB - 1, before)
    extra = jax.random.randint(key_extra, (bounds,), 0, MAXB)
    length = before + 1 + extra % (MAXB - before)
    length = jnp.where(which == reach, MAXB, length)
    starts_at = (which + 1) * group_blocks - before
    ends_at = starts_at + length
    index = jnp.arange(NBLOCKS)
    inside = jnp.any((index[:, None] > starts_at[None, :]) & (index[:, None] < ends_at[None, :]), axis=1)
    edge = jnp.any((index[:, None] == starts_at[None, :]) | (index[:, None] == ends_at[None, :]), axis=1)
    flags = jax.random.randint(key_flags, (NBLOCKS,), 0, 3) == 0
    flags = jnp.where(inside, False, jnp.where(edge, True, flags))
    flags = flags.at[0].set(True).at[NBLOCKS - 1].set(True)

    def walk(carry, item):
        current, run = carry
        flag, position = item
        begin = flag | (run >= MAXB)
        current = jnp.where(begin, position, current)
        run = jnp.where(begin, 1, run + 1)
        return ((current, run), current)
    _, starts = lax.scan(walk, (jnp.int32(0), jnp.int32(0)), (flags, index.astype(jnp.int32)))
    return (starts * BLOCK).astype(jnp.int32)


def shard_levels(key, dims, cuts, smallest, high):
    loudness, own = 1.0, jax.random.fold_in(key, 6)
    for dim, shards_of in cuts:
        heights = jnp.exp(jax.random.uniform(jax.random.fold_in(own, dim), (shards_of,), jnp.float32, smallest / len(cuts), high / len(cuts)))
        loudness = loudness * jnp.repeat(heights, dims[dim] // shards_of).reshape([-1 if axis == dim else 1 for axis in range(len(dims))])
    return loudness


def bell_draw(stream_key, shape, spread, most, shards=(), held_as=jnp.bfloat16):
    entries = spread * jax.random.normal(stream_key, shape, jnp.float32)
    if shards:
        entries = entries * shard_levels(stream_key, shape, shards, -0.22, 0.18)
    return jnp.clip(entries, -most, most).astype(held_as)


def setup_inputs(seed: int = 0) -> dict:
    key_list = jax.random.split(jax.random.key(seed), 6)
    return {
        "queries": draw_queries(jax.random.fold_in(key_list[5], 71), 0),
        "keys": draw_keys(jax.random.fold_in(key_list[5], 71), 0),
        "values": bell_draw(key_list[2], (SEQ, HEADS * HD), 1.0, 6.0, ((0, 256),)),
        "grad_out": bell_draw(key_list[3], (SEQ, HEADS * HD), 1.0, 6.0, ((0, 256),)),
        "doc_start": draw_doc_start(jax.random.fold_in(key_list[5], 71), 0),
    }


def head_grads(docs, arrays):
    q_head, k_head, v_head, d_head = arrays
    tile = 4 * BLOCK
    window = tile + MAXB * BLOCK
    scale = 1.0 / math.sqrt(HD)

    def step(carry, t):
        grad_k, grad_v = carry
        q_start = (t * tile).astype(jnp.int32)
        w_start = jnp.clip(q_start - MAXB * BLOCK, 0, SEQ - window).astype(jnp.int32)
        q_rows = lax.dynamic_slice_in_dim(q_head, q_start, tile, 0)
        d_rows = lax.dynamic_slice_in_dim(d_head, q_start, tile, 0)
        k_rows = lax.dynamic_slice_in_dim(k_head, w_start, window, 0)
        v_rows = lax.dynamic_slice_in_dim(v_head, w_start, window, 0)
        q_doc = lax.dynamic_slice_in_dim(docs, q_start, tile, 0)
        k_doc = lax.dynamic_slice_in_dim(docs, w_start, window, 0)
        q_pos = q_start + jnp.arange(tile, dtype=jnp.int32)
        k_pos = w_start + jnp.arange(window, dtype=jnp.int32)
        allowed = (q_doc[:, None] == k_doc[None, :]) & (k_pos[None, :] <= q_pos[:, None])
        score = jnp.dot(q_rows, k_rows.T, preferred_element_type=jnp.float32) * scale
        score = jnp.where(allowed, score, -jnp.inf)
        top = lax.optimization_barrier(jnp.max(score, axis=1, keepdims=True))
        lse = top + jnp.log(lax.optimization_barrier(jnp.sum(jnp.exp(score - top), axis=1, keepdims=True)))
        prob = jnp.exp(score - lse)
        dprob = jnp.dot(d_rows, v_rows.T, preferred_element_type=jnp.float32)
        delta = lax.optimization_barrier(jnp.sum(prob * dprob, axis=1, keepdims=True))
        dscore = (prob * (dprob - delta) * scale).astype(jnp.bfloat16)
        prob_low = prob.astype(jnp.bfloat16)
        grad_q = jnp.dot(dscore, k_rows, preferred_element_type=jnp.float32).astype(jnp.bfloat16)
        part_k = jnp.dot(dscore.T, q_rows, preferred_element_type=jnp.float32)
        part_v = jnp.dot(prob_low.T, d_rows, preferred_element_type=jnp.float32)
        grad_k = lax.dynamic_update_slice_in_dim(grad_k, lax.dynamic_slice_in_dim(grad_k, w_start, window, 0) + part_k, w_start, 0)
        grad_v = lax.dynamic_update_slice_in_dim(grad_v, lax.dynamic_slice_in_dim(grad_v, w_start, window, 0) + part_v, w_start, 0)
        return ((grad_k, grad_v), grad_q)
    start = (jnp.zeros((SEQ, HD), jnp.float32), jnp.zeros((SEQ, HD), jnp.float32))
    (grad_k, grad_v), grad_q = lax.scan(step, start, jnp.arange(SEQ // tile, dtype=jnp.int32))
    return (grad_q.reshape(SEQ, HD), grad_k.astype(jnp.bfloat16), grad_v.astype(jnp.bfloat16))

def reference(queries, keys, values, grad_out, doc_start):
    heads = queries.shape[1] // HD
    docs = jnp.repeat(doc_start, BLOCK)

    def split_heads(array):
        return array.reshape(SEQ, heads, HD).transpose(1, 0, 2)

    def merge_heads(array):
        return array.transpose(1, 0, 2).reshape(SEQ, heads * HD)
    grad_q, grad_k, grad_v = lax.map(partial(head_grads, docs), (split_heads(queries), split_heads(keys), split_heads(values), split_heads(grad_out)))
    return (merge_heads(grad_q), merge_heads(grad_k), merge_heads(grad_v))
```

```python
import functools
import math

import jax
import jax.numpy as jnp
from jax import lax
from jax.experimental import pallas as pl
from jax.experimental.pallas import tpu as pltpu
from jax.sharding import PartitionSpec as P

BLOCK = 128
MAXB = 8
REACH = MAXB - 1
EDGE = 8
MASKED = -1e30
LOG2E = 1.4426950408889634
F32 = jnp.float32
BF16 = jnp.bfloat16
QUERY, DOUT, KEY, VALUE = 0, 1, 2, 3
GKEY, GVALUE, GQUERY = 0, 1, 2


def across(a, b):
    return lax.dot_general(a, b, (((1,), (1,)), ((), ())), preferred_element_type=F32)


def down(a, b):
    return lax.dot_general(a, b, (((0,), (0,)), ((), ())), preferred_element_type=F32)


def plain(a, b):
    return jnp.dot(a, b, preferred_element_type=F32)


def query_pair(n, lead, second, q, d, k, v):
    width = q.shape[-1]
    scale = 1.0 / math.sqrt(width)
    rows = n * BLOCK
    s = across(k, q)
    r = lax.broadcasted_iota(jnp.int32, (rows, 2 * BLOCK), 0)
    c = lax.broadcasted_iota(jnp.int32, (1, 2 * BLOCK), 1)
    low = jnp.where(c < BLOCK, 0, second * BLOCK)
    high = c + (n - 2) * BLOCK
    s = jnp.where((r >= low) & (r <= high), s, MASKED)
    top = jnp.max(s, axis=0, keepdims=True)
    w = jnp.exp2((s - top) * (scale * LOG2E))
    total = jnp.sum(w, axis=0, keepdims=True)
    dp = across(v, d)
    cross = jnp.sum(w * dp, axis=0, keepdims=True)
    inv = 1.0 / total
    delta = cross * inv
    prob = w * inv
    ds = (prob * (dp - delta) * scale).astype(BF16)
    gv = plain(prob.astype(BF16), d)
    gk = plain(ds, q)
    gq = down(ds, k)
    lse = top * (scale * LOG2E) + jnp.log2(total)
    return gq, gk, gv, lse, delta


def inner_kernel(st_ref, x_ref, out_ref, head_ref, tail_ref, gk_ref, gv_ref):
    blocks = x_ref.shape[0]
    width = x_ref.shape[-1]
    gk_ref[...] = jnp.zeros_like(gk_ref)
    gv_ref[...] = jnp.zeros_like(gv_ref)

    def tile(t, _):
        first = st_ref[2 * t]
        n_dyn = 2 * t + 2 - first
        second = st_ref[2 * t + 1] - first
        for n in range(2, MAXB + 2):

            @pl.when((first >= 0) & (n_dyn == n))
            def _():
                window = pl.ds(first, n)
                pair = pl.ds(2 * t, 2)
                gq, gk, gv, _, _ = query_pair(
                    n,
                    0,
                    second,
                    x_ref[pair, QUERY].reshape(2 * BLOCK, width),
                    x_ref[pair, DOUT].reshape(2 * BLOCK, width),
                    x_ref[window, KEY].reshape(n * BLOCK, width),
                    x_ref[window, VALUE].reshape(n * BLOCK, width),
                )
                gk_ref[window] += gk.reshape(n, BLOCK, width)
                gv_ref[window] += gv.reshape(n, BLOCK, width)
                out_ref[pair, GQUERY] = gq.astype(BF16).reshape(2, BLOCK, width)

        return 0

    lax.fori_loop(0, blocks // 2, tile, 0)

    def store(i, _):
        out_ref[i, GKEY] = gk_ref[i].astype(BF16)
        out_ref[i, GVALUE] = gv_ref[i].astype(BF16)
        return 0

    lax.fori_loop(0, blocks, store, 0)
    head_ref[:, GKEY] = gk_ref[:EDGE]
    head_ref[:, GVALUE] = gv_ref[:EDGE]
    tail_ref[:, GKEY] = gk_ref[blocks - EDGE :]
    tail_ref[:, GVALUE] = gv_ref[blocks - EDGE :]


def head_kernel(
    st_ref, x_ref, far_ref, head_ref, out_in_ref, out_ref, stat_ref, k_ref, v_ref, gk_ref, gv_ref
):
    width = x_ref.shape[-1]
    k_ref[:REACH] = far_ref[:, 0]
    v_ref[:REACH] = far_ref[:, 1]
    k_ref[REACH:] = x_ref[:, KEY]
    v_ref[REACH:] = x_ref[:, VALUE]
    gk_ref[REACH:] = head_ref[:, GKEY]
    gv_ref[REACH:] = head_ref[:, GVALUE]
    out_ref[:, GQUERY] = out_in_ref[:, GQUERY]
    stat_ref[...] = jnp.full(stat_ref.shape, -MASKED, F32)

    def tile(t, _):
        first = st_ref[2 * t]
        n_dyn = 2 * t + 2 - first
        second = st_ref[2 * t + 1] - first
        for n in range(3, MAXB + 2):

            @pl.when((first < 0) & (n_dyn == n))
            def _():
                window = pl.ds(first + REACH, n)
                pair = pl.ds(2 * t, 2)
                gq, gk, gv, lse, delta = query_pair(
                    n,
                    0,
                    second,
                    x_ref[pair, QUERY].reshape(2 * BLOCK, width),
                    x_ref[pair, DOUT].reshape(2 * BLOCK, width),
                    k_ref[window].reshape(n * BLOCK, width),
                    v_ref[window].reshape(n * BLOCK, width),
                )
                gk_ref[window] += gk.reshape(n, BLOCK, width)
                gv_ref[window] += gv.reshape(n, BLOCK, width)
                out_ref[pair, GQUERY] = gq.astype(BF16).reshape(2, BLOCK, width)
                c = lax.broadcasted_iota(jnp.int32, lse.shape, 1)
                lse = jnp.where((c < BLOCK) | (second == 0), lse, -MASKED)
                stat_ref[t, 0:1, :] = lse
                stat_ref[t, 1:2, :] = delta

        return 0

    lax.fori_loop(0, EDGE // 2, tile, 0)
    out_ref[:, GKEY] = gk_ref[REACH:].astype(BF16)
    out_ref[:, GVALUE] = gv_ref[REACH:].astype(BF16)


def tail_kernel(st_ref, x_ref, near_ref, stat_ref, tail_ref, out_in_ref, out_ref, gk_ref, gv_ref):
    del out_in_ref
    width = x_ref.shape[-1]
    scale = 1.0 / math.sqrt(width)
    gk_ref[...] = tail_ref[:, GKEY]
    gv_ref[...] = tail_ref[:, GVALUE]
    rows = REACH * BLOCK
    q = near_ref[:, 0].reshape(rows, width)
    d = near_ref[:, 1].reshape(rows, width)
    lse = jnp.concatenate([stat_ref[t, 0:1, :] for t in range(EDGE // 2)], 1)[:, :rows]
    delta = jnp.concatenate([stat_ref[t, 1:2, :] for t in range(EDGE // 2)], 1)[:, :rows]
    live = lse < -MASKED
    delta = jnp.where(live, delta, 0.0)

    def key_block(j, _):
        s = across(x_ref[j, KEY], q)
        dp = across(x_ref[j, VALUE], d)
        prob = jnp.exp2(s * (scale * LOG2E) - lse)
        ds = (prob * (dp - delta) * scale).astype(BF16)
        gv_ref[j] += plain(prob.astype(BF16), d)
        gk_ref[j] += plain(ds, q)
        return 0

    lax.fori_loop(st_ref[st_ref.shape[0] - 1], EDGE, key_block, 0)
    out_ref[:, GKEY] = gk_ref[...].astype(BF16)
    out_ref[:, GVALUE] = gv_ref[...].astype(BF16)


def whole():
    return pl.BlockSpec(memory_space=pltpu.VMEM)


def passed_along(array, axis, by):
    devices = lax.axis_size(axis)
    pairs = [(i, i + by) for i in range(devices) if 0 <= i + by < devices]
    return lax.ppermute(array, axis, pairs)


def body(queries, keys, values, grad_out, doc_start):
    ulys = lax.axis_size("uly")
    rows, columns = queries.shape
    width = columns // ulys
    blocks = ulys * rows // BLOCK
    group = lax.axis_index("blk")
    last = lax.axis_size("blk") - 1

    packed = jnp.stack(
        [a.reshape(rows, ulys, width) for a in (queries, grad_out, keys, values)], 0
    ).transpose(2, 0, 1, 3)
    x = lax.all_to_all(packed, "uly", split_axis=0, concat_axis=0, tiled=True)

    own = lax.dynamic_slice_in_dim(doc_start, group * blocks, blocks, 0) // BLOCK - group * blocks
    after = lax.dynamic_slice_in_dim(doc_start, jnp.minimum(group + 1, last) * blocks, 1, 0) // BLOCK
    after = jnp.where(group == last, EDGE, after - group * blocks - (blocks - EDGE))
    starts = jnp.concatenate([own, after]).astype(jnp.int32)

    far = passed_along(x[blocks - REACH :, KEY : VALUE + 1], "blk", 1)
    near = passed_along(x[:REACH, QUERY : DOUT + 1], "blk", -1)

    smem = pl.BlockSpec(memory_space=pltpu.SMEM)
    params = pltpu.CompilerParams(vmem_limit_bytes=48 * 1024 * 1024)
    tile_shape = (BLOCK, width)
    out_type = jax.ShapeDtypeStruct((blocks, 3) + tile_shape, BF16)
    edge_type = jax.ShapeDtypeStruct((EDGE, 2) + tile_shape, F32)
    out, head_acc, tail_acc = pl.pallas_call(
        inner_kernel,
        out_shape=(out_type, edge_type, edge_type),
        in_specs=[smem, whole()],
        out_specs=(whole(), whole(), whole()),
        scratch_shapes=[pltpu.VMEM((blocks,) + tile_shape, F32)] * 2,
        compiler_params=params,
        cost_estimate=pl.CostEstimate(
            flops=10 * 120 * BLOCK**3 * 4, bytes_accessed=9 << 20, transcendentals=120 << 14
        ),
        name="inner",
    )(starts, x)

    def edge_in(kinds, at):
        return pl.BlockSpec((EDGE, kinds) + tile_shape, lambda i: (at, 0, 0, 0))

    def full(shape):
        return pl.BlockSpec(shape, lambda i: (0,) * len(shape))

    stat_shape = (EDGE // 2, 8, 2 * BLOCK)
    out, stats = pl.pallas_call(
        head_kernel,
        grid=(1,),
        out_shape=(out_type, jax.ShapeDtypeStruct(stat_shape, F32)),
        in_specs=[
            smem,
            edge_in(4, 0),
            full((REACH, 2) + tile_shape),
            full((EDGE, 2) + tile_shape),
            edge_in(3, 0),
        ],
        out_specs=(edge_in(3, 0), full(stat_shape)),
        scratch_shapes=[pltpu.VMEM((REACH + EDGE,) + tile_shape, BF16)] * 2
        + [pltpu.VMEM((REACH + EDGE,) + tile_shape, F32)] * 2,
        input_output_aliases={4: 0},
        compiler_params=params,
        name="head",
    )(starts, x, far, head_acc, out)
    stats = passed_along(stats, "blk", -1)
    at_end = blocks // EDGE - 1
    out = pl.pallas_call(
        tail_kernel,
        grid=(1,),
        out_shape=out_type,
        in_specs=[
            smem,
            edge_in(4, at_end),
            full((REACH, 2) + tile_shape),
            full(stat_shape),
            full((EDGE, 2) + tile_shape),
            pl.BlockSpec(memory_space=pl.ANY),
        ],
        out_specs=edge_in(2, at_end),
        scratch_shapes=[pltpu.VMEM((EDGE,) + tile_shape, F32)] * 2,
        input_output_aliases={5: 0},
        compiler_params=params,
        name="tail",
    )(starts, x, near, stats, tail_acc, out)

    back = lax.all_to_all(out, "uly", split_axis=0, concat_axis=0, tiled=True)
    back = back.transpose(1, 2, 0, 3).reshape(3, rows, columns)
    return back[GQUERY], back[GKEY], back[GVALUE]


def solution(mesh):
    part = P(("blk", "uly"), None)
    return jax.shard_map(
        body,
        mesh=mesh,
        in_specs=(part, part, part, part, P()),
        out_specs=(part, part, part),
        check_vma=False,
    )
```

```python
import functools
import math

import jax
import jax.numpy as jnp
from jax import lax
from jax.experimental import pallas as pl
from jax.experimental.pallas import tpu as pltpu
from jax.sharding import PartitionSpec as P

BLOCK = 128
MAXB = 8
REACH = MAXB - 1
EDGE = 8
MASKED = -1e30
LOG2E = 1.4426950408889634
F32 = jnp.float32
BF16 = jnp.bfloat16
QUERY, DOUT, KEY, VALUE = 0, 1, 2, 3
GKEY, GVALUE, GQUERY = 0, 1, 2


def across(a, b):
    return lax.dot_general(a, b, (((1,), (1,)), ((), ())), preferred_element_type=F32)


def down(a, b):
    return lax.dot_general(a, b, (((0,), (0,)), ((), ())), preferred_element_type=F32)


def plain(a, b):
    return jnp.dot(a, b, preferred_element_type=F32)


def query_pair(n, lead, second, q, d, k, v):
    width = q.shape[-1]
    scale = 1.0 / math.sqrt(width)
    rows = n * BLOCK
    s = across(k, q)
    r = lax.broadcasted_iota(jnp.int32, (rows, 2 * BLOCK), 0)
    c = lax.broadcasted_iota(jnp.int32, (1, 2 * BLOCK), 1)
    low = jnp.where(c < BLOCK, 0, second * BLOCK)
    high = c + (n - 2) * BLOCK
    s = jnp.where((r >= low) & (r <= high), s, MASKED)
    top = jnp.max(s, axis=0, keepdims=True)
    w = jnp.exp2((s - top) * (scale * LOG2E))
    total = jnp.sum(w, axis=0, keepdims=True)
    dp = across(v, d)
    cross = jnp.sum(w * dp, axis=0, keepdims=True)
    inv = 1.0 / total
    delta = cross * inv
    prob = w * inv
    ds = (prob * (dp - delta) * scale).astype(BF16)
    gv = plain(prob.astype(BF16), d)
    gk = plain(ds, q)
    gq = down(ds, k)
    lse = top * (scale * LOG2E) + jnp.log2(total)
    return gq, gk, gv, lse, delta


def inner_kernel(st_ref, x_ref, out_ref, head_ref, tail_ref, gk_ref, gv_ref):
    blocks = x_ref.shape[0]
    width = x_ref.shape[-1]
    gk_ref[...] = jnp.zeros_like(gk_ref)
    gv_ref[...] = jnp.zeros_like(gv_ref)

    def tile(t, _):
        first = st_ref[2 * t]
        n_dyn = 2 * t + 2 - first
        second = st_ref[2 * t + 1] - first
        for n in range(2, MAXB + 2):

            @pl.when((first >= 0) & (n_dyn == n))
            def _():
                window = pl.ds(first, n)
                pair = pl.ds(2 * t, 2)
                gq, gk, gv, _, _ = query_pair(
                    n,
                    0,
                    second,
                    x_ref[pair, QUERY].reshape(2 * BLOCK, width),
                    x_ref[pair, DOUT].reshape(2 * BLOCK, width),
                    x_ref[window, KEY].reshape(n * BLOCK, width),
                    x_ref[window, VALUE].reshape(n * BLOCK, width),
                )
                gk_ref[window] += gk.reshape(n, BLOCK, width)
                gv_ref[window] += gv.reshape(n, BLOCK, width)
                out_ref[pair, GQUERY] = gq.astype(BF16).reshape(2, BLOCK, width)

        return 0

    lax.fori_loop(0, blocks // 2, tile, 0)

    def store(i, _):
        out_ref[i, GKEY] = gk_ref[i].astype(BF16)
        out_ref[i, GVALUE] = gv_ref[i].astype(BF16)
        return 0

    lax.fori_loop(0, blocks, store, 0)
    head_ref[:, GKEY] = gk_ref[:EDGE]
    head_ref[:, GVALUE] = gv_ref[:EDGE]
    tail_ref[:, GKEY] = gk_ref[blocks - EDGE :]
    tail_ref[:, GVALUE] = gv_ref[blocks - EDGE :]


def head_kernel(
    st_ref, x_ref, far_ref, head_ref, out_in_ref, out_ref, stat_ref, k_ref, v_ref, gk_ref, gv_ref
):
    width = x_ref.shape[-1]
    k_ref[:REACH] = far_ref[:, 0]
    v_ref[:REACH] = far_ref[:, 1]
    k_ref[REACH:] = x_ref[:, KEY]
    v_ref[REACH:] = x_ref[:, VALUE]
    gk_ref[REACH:] = head_ref[:, GKEY]
    gv_ref[REACH:] = head_ref[:, GVALUE]
    out_ref[:, GQUERY] = out_in_ref[:, GQUERY]
    stat_ref[...] = jnp.full(stat_ref.shape, -MASKED, F32)

    def tile(t, _):
        first = st_ref[2 * t]
        n_dyn = 2 * t + 2 - first
        second = st_ref[2 * t + 1] - first
        for n in range(3, MAXB + 2):

            @pl.when((first < 0) & (n_dyn == n))
            def _():
                window = pl.ds(first + REACH, n)
                pair = pl.ds(2 * t, 2)
                gq, gk, gv, lse, delta = query_pair(
                    n,
                    0,
                    second,
                    x_ref[pair, QUERY].reshape(2 * BLOCK, width),
                    x_ref[pair, DOUT].reshape(2 * BLOCK, width),
                    k_ref[window].reshape(n * BLOCK, width),
                    v_ref[window].reshape(n * BLOCK, width),
                )
                gk_ref[window] += gk.reshape(n, BLOCK, width)
                gv_ref[window] += gv.reshape(n, BLOCK, width)
                out_ref[pair, GQUERY] = gq.astype(BF16).reshape(2, BLOCK, width)
                c = lax.broadcasted_iota(jnp.int32, lse.shape, 1)
                lse = jnp.where((c < BLOCK) | (second == 0), lse, -MASKED)
                stat_ref[t, 0:1, :] = lse
                stat_ref[t, 1:2, :] = delta

        return 0

    lax.fori_loop(0, EDGE // 2, tile, 0)
    out_ref[:, GKEY] = gk_ref[REACH:].astype(BF16)
    out_ref[:, GVALUE] = gv_ref[REACH:].astype(BF16)


def tail_kernel(st_ref, x_ref, near_ref, stat_ref, tail_ref, out_in_ref, out_ref, gk_ref, gv_ref):
    del out_in_ref
    width = x_ref.shape[-1]
    scale = 1.0 / math.sqrt(width)
    gk_ref[...] = tail_ref[:, GKEY]
    gv_ref[...] = tail_ref[:, GVALUE]
    rows = REACH * BLOCK
    q = near_ref[:, 0].reshape(rows, width)
    d = near_ref[:, 1].reshape(rows, width)
    lse = jnp.concatenate([stat_ref[t, 0:1, :] for t in range(EDGE // 2)], 1)[:, :rows]
    delta = jnp.concatenate([stat_ref[t, 1:2, :] for t in range(EDGE // 2)], 1)[:, :rows]
    live = lse < -MASKED
    delta = jnp.where(live, delta, 0.0)

    def key_block(j, _):
        s = across(x_ref[j, KEY], q)
        dp = across(x_ref[j, VALUE], d)
        prob = jnp.exp2(s * (scale * LOG2E) - lse)
        ds = (prob * (dp - delta) * scale).astype(BF16)
        gv_ref[j] += plain(prob.astype(BF16), d)
        gk_ref[j] += plain(ds, q)
        return 0

    lax.fori_loop(st_ref[st_ref.shape[0] - 1], EDGE, key_block, 0)
    out_ref[:, GKEY] = gk_ref[...].astype(BF16)
    out_ref[:, GVALUE] = gv_ref[...].astype(BF16)


def pack_kernel(*refs):
    *arrays, out_ref = refs
    heads, _, _, width = out_ref.shape
    for kind, array in enumerate(arrays):
        for h in range(heads):
            out_ref[h, kind] = array[:, h * width : (h + 1) * width]


def unpack_kernel(back_ref, *refs):
    heads, kinds, _, width = back_ref.shape
    for kind, out in enumerate(refs[len(refs) - kinds :]):
        for h in range(heads):
            out[:, h * width : (h + 1) * width] = back_ref[h, kind]


def whole():
    return pl.BlockSpec(memory_space=pltpu.VMEM)


SMEM = pl.BlockSpec(memory_space=pltpu.SMEM)
PARAMS = pltpu.CompilerParams(vmem_limit_bytes=40 * 1024 * 1024)
PACK_PARAMS = pltpu.CompilerParams(vmem_limit_bytes=60 * 1024 * 1024)
STEP = 4


def packed(arrays, half, heads):
    rows, columns = arrays[0].shape
    width = columns // (PHASES * heads)
    steps = heads // STEP
    return pl.pallas_call(
        pack_kernel,
        grid=(steps,),
        out_shape=jax.ShapeDtypeStruct((heads, len(arrays), rows, width), BF16),
        in_specs=[pl.BlockSpec((rows, STEP * width), lambda i: (0, half * steps + i))] * len(arrays),
        out_specs=pl.BlockSpec((STEP, len(arrays), rows, width), lambda i: (i, 0, 0, 0)),
        compiler_params=PACK_PARAMS,
        cost_estimate=pl.CostEstimate(flops=0, bytes_accessed=4 << 20, transcendentals=0),
        name="pack",
    )(*arrays)


def unpacked(back, half, before):
    heads, kinds, rows, width = back.shape
    steps = heads // STEP
    shape = jax.ShapeDtypeStruct((rows, PHASES * heads * width), BF16)
    return pl.pallas_call(
        unpack_kernel,
        grid=(steps,),
        out_shape=(shape,) * kinds,
        in_specs=[pl.BlockSpec((STEP, kinds, rows, width), lambda i: (i, 0, 0, 0))]
        + [pl.BlockSpec(memory_space=pl.ANY)] * len(before),
        out_specs=(pl.BlockSpec((rows, STEP * width), lambda i: (0, half * steps + i)),) * kinds,
        input_output_aliases={1 + i: i for i in range(len(before))},
        compiler_params=PARAMS,
        cost_estimate=pl.CostEstimate(flops=0, bytes_accessed=3 << 20, transcendentals=0),
        name="unpack",
    )(back, *before)


def passed_along(array, by):
    devices = lax.axis_size(("blk", "uly"))
    pairs = [(i, i + by) for i in range(devices) if 0 <= i + by < devices]
    return lax.ppermute(array, ("blk", "uly"), pairs)


def head_grads(starts, x, heads):
    blocks = x.shape[0]
    tile_shape = x.shape[2:]
    far = passed_along(x[blocks - REACH :, KEY : VALUE + 1], heads)
    near = passed_along(x[:REACH, QUERY : DOUT + 1], -heads)
    out_type = jax.ShapeDtypeStruct((blocks, 3) + tile_shape, BF16)
    edge_type = jax.ShapeDtypeStruct((EDGE, 2) + tile_shape, F32)
    out, head_acc, tail_acc = pl.pallas_call(
        inner_kernel,
        out_shape=(out_type, edge_type, edge_type),
        in_specs=[SMEM, whole()],
        out_specs=(whole(), whole(), whole()),
        scratch_shapes=[pltpu.VMEM((blocks,) + tile_shape, F32)] * 2,
        compiler_params=PARAMS,
        cost_estimate=pl.CostEstimate(flops=8 * 10**9, bytes_accessed=6 << 20, transcendentals=1 << 20),
        name="inner",
    )(starts, x)

    def edge_in(kinds, at):
        return pl.BlockSpec((EDGE, kinds) + tile_shape, lambda i: (at, 0, 0, 0))

    def full(shape):
        return pl.BlockSpec(shape, lambda i: (0,) * len(shape))

    stat_shape = (EDGE // 2, 8, 2 * BLOCK)
    out, stats = pl.pallas_call(
        head_kernel,
        grid=(1,),
        out_shape=(out_type, jax.ShapeDtypeStruct(stat_shape, F32)),
        in_specs=[
            SMEM,
            edge_in(4, 0),
            full((REACH, 2) + tile_shape),
            full((EDGE, 2) + tile_shape),
            edge_in(3, 0),
        ],
        out_specs=(edge_in(3, 0), full(stat_shape)),
        scratch_shapes=[pltpu.VMEM((REACH + EDGE,) + tile_shape, BF16)] * 2
        + [pltpu.VMEM((REACH + EDGE,) + tile_shape, F32)] * 2,
        input_output_aliases={4: 0},
        compiler_params=PARAMS,
        cost_estimate=pl.CostEstimate(flops=2 * 10**9, bytes_accessed=3 << 20, transcendentals=1 << 18),
        name="head",
    )(starts, x, far, head_acc, out)
    stats = passed_along(stats, -heads)
    at_end = blocks // EDGE - 1
    return pl.pallas_call(
        tail_kernel,
        grid=(1,),
        out_shape=out_type,
        in_specs=[
            SMEM,
            edge_in(4, at_end),
            full((REACH, 2) + tile_shape),
            full(stat_shape),
            full((EDGE, 2) + tile_shape),
            pl.BlockSpec(memory_space=pl.ANY),
        ],
        out_specs=edge_in(2, at_end),
        scratch_shapes=[pltpu.VMEM((EDGE,) + tile_shape, F32)] * 2,
        input_output_aliases={5: 0},
        compiler_params=PARAMS,
        cost_estimate=pl.CostEstimate(flops=2 * 10**9, bytes_accessed=3 << 20, transcendentals=1 << 18),
        name="tail",
    )(starts, x, near, stats, tail_acc, out)


PHASES = 2


def body(queries, keys, values, grad_out, doc_start):
    ulys = lax.axis_size("uly")
    heads = ulys // PHASES
    groups = [list(range(g * heads, (g + 1) * heads)) for g in range(PHASES)]

    blocks = heads * queries.shape[0] // BLOCK
    segment = lax.axis_index("blk") * PHASES + lax.axis_index("uly") // heads
    last = lax.axis_size("blk") * PHASES - 1
    own = lax.dynamic_slice_in_dim(doc_start, segment * blocks, blocks, 0) // BLOCK - segment * blocks
    after = lax.dynamic_slice_in_dim(doc_start, jnp.minimum(segment + 1, last) * blocks, 1, 0) // BLOCK
    after = jnp.where(segment == last, EDGE, after - segment * blocks - (blocks - EDGE))
    starts = jnp.concatenate([own, after]).astype(jnp.int32)

    def exchanged(array):
        return lax.all_to_all(
            array, "uly", split_axis=0, concat_axis=0, tiled=True, axis_index_groups=groups
        )

    arrays = (queries, grad_out, keys, values)
    inputs = [exchanged(packed(arrays, p, heads)) for p in range(PHASES)]
    grads = [exchanged(head_grads(starts, x, heads)) for x in inputs]
    outs = ()
    for p in range(PHASES):
        outs = unpacked(grads[p], p, outs)
    return outs[GQUERY], outs[GKEY], outs[GVALUE]


def solution(mesh):
    part = P(("blk", "uly"), None)
    return jax.shard_map(
        body,
        mesh=mesh,
        in_specs=(part, part, part, part, P()),
        out_specs=(part, part, part),
        check_vma=False,
    )
```

```python
import functools
import math

import jax
import jax.numpy as jnp
from jax import lax
from jax.experimental import pallas as pl
from jax.experimental.pallas import tpu as pltpu
from jax.sharding import PartitionSpec as P

BLOCK = 128
MAXB = 8
REACH = MAXB - 1
EDGE = 8
MASKED = -1e30
LOG2E = 1.4426950408889634
F32 = jnp.float32
BF16 = jnp.bfloat16
QUERY, DOUT, KEY, VALUE = 0, 1, 2, 3
GKEY, GVALUE, GQUERY = 0, 1, 2


def across(a, b):
    return lax.dot_general(a, b, (((1,), (1,)), ((), ())), preferred_element_type=F32)


def down(a, b):
    return lax.dot_general(a, b, (((0,), (0,)), ((), ())), preferred_element_type=F32)


def plain(a, b):
    return jnp.dot(a, b, preferred_element_type=F32)


def query_pair(n, lead, second, q, d, k, v):
    width = q.shape[-1]
    scale = 1.0 / math.sqrt(width)
    rows = n * BLOCK
    s = across(k, q)
    r = lax.broadcasted_iota(jnp.int32, (rows, 2 * BLOCK), 0)
    c = lax.broadcasted_iota(jnp.int32, (1, 2 * BLOCK), 1)
    low = jnp.where(c < BLOCK, 0, second * BLOCK)
    high = c + (n - 2) * BLOCK
    s = jnp.where((r >= low) & (r <= high), s, MASKED)
    top = jnp.max(s, axis=0, keepdims=True)
    w = jnp.exp2((s - top) * (scale * LOG2E))
    total = jnp.sum(w, axis=0, keepdims=True)
    dp = across(v, d)
    cross = jnp.sum(w * dp, axis=0, keepdims=True)
    inv = 1.0 / total
    delta = cross * inv
    prob = w * inv
    ds = (prob * (dp - delta) * scale).astype(BF16)
    gv = plain(prob.astype(BF16), d)
    gk = plain(ds, q)
    gq = down(ds, k)
    lse = top * (scale * LOG2E) + jnp.log2(total)
    return gq, gk, gv, lse, delta


def inner_kernel(st_ref, x_ref, out_ref, head_ref, tail_ref, near_ref, gk_ref, gv_ref):
    blocks = x_ref.shape[0]
    width = x_ref.shape[-1]
    gk_ref[...] = jnp.zeros_like(gk_ref)
    gv_ref[...] = jnp.zeros_like(gv_ref)
    near_ref[...] = x_ref[:REACH, QUERY : DOUT + 1]

    def tile(t, _):
        first = st_ref[2 * t]
        n_dyn = 2 * t + 2 - first
        second = st_ref[2 * t + 1] - first
        for n in range(2, MAXB + 2):

            @pl.when((first >= 0) & (n_dyn == n))
            def _():
                window = pl.ds(first, n)
                pair = pl.ds(2 * t, 2)
                gq, gk, gv, _, _ = query_pair(
                    n,
                    0,
                    second,
                    x_ref[pair, QUERY].reshape(2 * BLOCK, width),
                    x_ref[pair, DOUT].reshape(2 * BLOCK, width),
                    x_ref[window, KEY].reshape(n * BLOCK, width),
                    x_ref[window, VALUE].reshape(n * BLOCK, width),
                )
                gk_ref[window] += gk.reshape(n, BLOCK, width)
                gv_ref[window] += gv.reshape(n, BLOCK, width)
                out_ref[pair, GQUERY] = gq.astype(BF16).reshape(2, BLOCK, width)

        return 0

    lax.fori_loop(0, blocks // 2, tile, 0)

    def store(i, _):
        out_ref[i, GKEY] = gk_ref[i].astype(BF16)
        out_ref[i, GVALUE] = gv_ref[i].astype(BF16)
        return 0

    lax.fori_loop(0, blocks, store, 0)
    head_ref[:, GKEY] = gk_ref[:EDGE]
    head_ref[:, GVALUE] = gv_ref[:EDGE]
    tail_ref[:, GKEY] = gk_ref[blocks - EDGE :]
    tail_ref[:, GVALUE] = gv_ref[blocks - EDGE :]


def head_kernel(
    st_ref, x_ref, far_ref, head_ref, out_in_ref, out_ref, stat_ref, k_ref, v_ref, gk_ref, gv_ref
):
    width = x_ref.shape[-1]
    k_ref[:REACH] = far_ref[:, 0]
    v_ref[:REACH] = far_ref[:, 1]
    k_ref[REACH:] = x_ref[:, KEY]
    v_ref[REACH:] = x_ref[:, VALUE]
    gk_ref[REACH:] = head_ref[:, GKEY]
    gv_ref[REACH:] = head_ref[:, GVALUE]
    out_ref[:, GQUERY] = out_in_ref[:, GQUERY]
    stat_ref[...] = jnp.full(stat_ref.shape, -MASKED, F32)

    def tile(t, _):
        first = st_ref[2 * t]
        n_dyn = 2 * t + 2 - first
        second = st_ref[2 * t + 1] - first
        for n in range(3, MAXB + 2):

            @pl.when((first < 0) & (n_dyn == n))
            def _():
                window = pl.ds(first + REACH, n)
                pair = pl.ds(2 * t, 2)
                gq, gk, gv, lse, delta = query_pair(
                    n,
                    0,
                    second,
                    x_ref[pair, QUERY].reshape(2 * BLOCK, width),
                    x_ref[pair, DOUT].reshape(2 * BLOCK, width),
                    k_ref[window].reshape(n * BLOCK, width),
                    v_ref[window].reshape(n * BLOCK, width),
                )
                gk_ref[window] += gk.reshape(n, BLOCK, width)
                gv_ref[window] += gv.reshape(n, BLOCK, width)
                out_ref[pair, GQUERY] = gq.astype(BF16).reshape(2, BLOCK, width)
                c = lax.broadcasted_iota(jnp.int32, lse.shape, 1)
                lse = jnp.where((c < BLOCK) | (second == 0), lse, -MASKED)
                stat_ref[t, 0:1, :] = lse
                stat_ref[t, 1:2, :] = delta

        return 0

    lax.fori_loop(0, EDGE // 2, tile, 0)
    out_ref[:, GKEY] = gk_ref[REACH:].astype(BF16)
    out_ref[:, GVALUE] = gv_ref[REACH:].astype(BF16)


def tail_kernel(st_ref, x_ref, near_ref, stat_ref, tail_ref, out_in_ref, out_ref, gk_ref, gv_ref):
    del out_in_ref
    width = x_ref.shape[-1]
    scale = 1.0 / math.sqrt(width)
    gk_ref[...] = tail_ref[:, GKEY]
    gv_ref[...] = tail_ref[:, GVALUE]
    rows = REACH * BLOCK
    q = near_ref[:, 0].reshape(rows, width)
    d = near_ref[:, 1].reshape(rows, width)
    lse = jnp.concatenate([stat_ref[t, 0:1, :] for t in range(EDGE // 2)], 1)[:, :rows]
    delta = jnp.concatenate([stat_ref[t, 1:2, :] for t in range(EDGE // 2)], 1)[:, :rows]
    live = lse < -MASKED
    delta = jnp.where(live, delta, 0.0)

    def key_block(j, _):
        s = across(x_ref[j, KEY], q)
        dp = across(x_ref[j, VALUE], d)
        prob = jnp.exp2(s * (scale * LOG2E) - lse)
        ds = (prob * (dp - delta) * scale).astype(BF16)
        gv_ref[j] += plain(prob.astype(BF16), d)
        gk_ref[j] += plain(ds, q)
        return 0

    lax.fori_loop(st_ref[st_ref.shape[0] - 1], EDGE, key_block, 0)
    out_ref[:, GKEY] = gk_ref[...].astype(BF16)
    out_ref[:, GVALUE] = gv_ref[...].astype(BF16)


def pack_kernel(*refs):
    *arrays, out_ref = refs
    heads, _, _, width = out_ref.shape
    for kind, array in enumerate(arrays):
        for h in range(heads):
            out_ref[h, kind] = array[:, h * width : (h + 1) * width]


def unpack_kernel(back_ref, *refs):
    heads, kinds, _, width = back_ref.shape
    for kind, out in enumerate(refs[len(refs) - kinds :]):
        for h in range(heads):
            out[:, h * width : (h + 1) * width] = back_ref[h, kind]


def whole():
    return pl.BlockSpec(memory_space=pltpu.VMEM)


SMEM = pl.BlockSpec(memory_space=pltpu.SMEM)
PARAMS = pltpu.CompilerParams(vmem_limit_bytes=40 * 1024 * 1024)
PACK_PARAMS = pltpu.CompilerParams(vmem_limit_bytes=60 * 1024 * 1024)
STEP = 16


def packed(arrays, half, heads):
    rows, columns = arrays[0].shape
    width = columns // (PHASES * heads)
    steps = heads // STEP
    return pl.pallas_call(
        pack_kernel,
        grid=(steps,),
        out_shape=jax.ShapeDtypeStruct((heads, len(arrays), rows, width), BF16),
        in_specs=[pl.BlockSpec((rows, STEP * width), lambda i: (0, half * steps + i))] * len(arrays),
        out_specs=pl.BlockSpec((STEP, len(arrays), rows, width), lambda i: (i, 0, 0, 0)),
        compiler_params=PACK_PARAMS,
        cost_estimate=pl.CostEstimate(flops=0, bytes_accessed=4 << 20, transcendentals=0),
        name="pack",
    )(*arrays)


def unpacked(back, half, before):
    heads, kinds, rows, width = back.shape
    steps = heads // STEP
    shape = jax.ShapeDtypeStruct((rows, PHASES * heads * width), BF16)
    return pl.pallas_call(
        unpack_kernel,
        grid=(steps,),
        out_shape=(shape,) * kinds,
        in_specs=[pl.BlockSpec((STEP, kinds, rows, width), lambda i: (i, 0, 0, 0))]
        + [pl.BlockSpec(memory_space=pl.ANY)] * len(before),
        out_specs=(pl.BlockSpec((rows, STEP * width), lambda i: (0, half * steps + i)),) * kinds,
        input_output_aliases={1 + i: i for i in range(len(before))},
        compiler_params=PARAMS,
        cost_estimate=pl.CostEstimate(flops=0, bytes_accessed=3 << 20, transcendentals=0),
        name="unpack",
    )(back, *before)


def passed_along(array, by):
    devices = lax.axis_size(("blk", "uly"))
    pairs = [(i, i + by) for i in range(devices) if 0 <= i + by < devices]
    return lax.ppermute(array, ("blk", "uly"), pairs)


def head_grads(starts, x, heads):
    blocks = x.shape[0]
    tile_shape = x.shape[2:]
    far = passed_along(x[blocks - REACH :, KEY : VALUE + 1], heads)
    out_type = jax.ShapeDtypeStruct((blocks, 3) + tile_shape, BF16)
    edge_type = jax.ShapeDtypeStruct((EDGE, 2) + tile_shape, F32)
    near_type = jax.ShapeDtypeStruct((REACH, 2) + tile_shape, BF16)
    out, head_acc, tail_acc, near = pl.pallas_call(
        inner_kernel,
        out_shape=(out_type, edge_type, edge_type, near_type),
        in_specs=[SMEM, whole()],
        out_specs=(whole(),) * 4,
        scratch_shapes=[pltpu.VMEM((blocks,) + tile_shape, F32)] * 2,
        compiler_params=PARAMS,
        cost_estimate=pl.CostEstimate(flops=8 * 10**9, bytes_accessed=6 << 20, transcendentals=1 << 20),
        name="inner",
    )(starts, x)

    def edge_in(kinds, at):
        return pl.BlockSpec((EDGE, kinds) + tile_shape, lambda i: (at, 0, 0, 0))

    def full(shape):
        return pl.BlockSpec(shape, lambda i: (0,) * len(shape))

    stat_shape = (EDGE // 2, 8, 2 * BLOCK)
    out, stats = pl.pallas_call(
        head_kernel,
        grid=(1,),
        out_shape=(out_type, jax.ShapeDtypeStruct(stat_shape, F32)),
        in_specs=[
            SMEM,
            edge_in(4, 0),
            full((REACH, 2) + tile_shape),
            full((EDGE, 2) + tile_shape),
            edge_in(3, 0),
        ],
        out_specs=(edge_in(3, 0), full(stat_shape)),
        scratch_shapes=[pltpu.VMEM((REACH + EDGE,) + tile_shape, BF16)] * 2
        + [pltpu.VMEM((REACH + EDGE,) + tile_shape, F32)] * 2,
        input_output_aliases={4: 0},
        compiler_params=PARAMS,
        cost_estimate=pl.CostEstimate(flops=2 * 10**9, bytes_accessed=3 << 20, transcendentals=1 << 18),
        name="head",
    )(starts, x, far, head_acc, out)
    stats = passed_along(stats, -heads)
    near = passed_along(near, -heads)
    at_end = blocks // EDGE - 1
    return pl.pallas_call(
        tail_kernel,
        grid=(1,),
        out_shape=out_type,
        in_specs=[
            SMEM,
            edge_in(4, at_end),
            full((REACH, 2) + tile_shape),
            full(stat_shape),
            full((EDGE, 2) + tile_shape),
            pl.BlockSpec(memory_space=pl.ANY),
        ],
        out_specs=edge_in(2, at_end),
        scratch_shapes=[pltpu.VMEM((EDGE,) + tile_shape, F32)] * 2,
        input_output_aliases={5: 0},
        compiler_params=PARAMS,
        cost_estimate=pl.CostEstimate(flops=2 * 10**9, bytes_accessed=3 << 20, transcendentals=1 << 18),
        name="tail",
    )(starts, x, near, stats, tail_acc, out)


PHASES = 2


def body(queries, keys, values, grad_out, doc_start):
    ulys = lax.axis_size("uly")
    heads = ulys // PHASES
    groups = [list(range(g * heads, (g + 1) * heads)) for g in range(PHASES)]

    blocks = heads * queries.shape[0] // BLOCK
    segment = lax.axis_index("blk") * PHASES + lax.axis_index("uly") // heads
    last = lax.axis_size("blk") * PHASES - 1
    own = lax.dynamic_slice_in_dim(doc_start, segment * blocks, blocks, 0) // BLOCK - segment * blocks
    after = lax.dynamic_slice_in_dim(doc_start, jnp.minimum(segment + 1, last) * blocks, 1, 0) // BLOCK
    after = jnp.where(segment == last, EDGE, after - segment * blocks - (blocks - EDGE))
    starts = jnp.concatenate([own, after]).astype(jnp.int32)

    def exchanged(array):
        return lax.all_to_all(
            array, "uly", split_axis=0, concat_axis=0, tiled=True, axis_index_groups=groups
        )

    arrays = (queries, grad_out, keys, values)
    inputs = [exchanged(packed(arrays, p, heads)) for p in range(PHASES)]
    grads = [exchanged(head_grads(starts, x, heads)) for x in inputs]
    outs = ()
    for p in range(PHASES):
        outs = unpacked(grads[p], p, outs)
    return outs[GQUERY], outs[GKEY], outs[GVALUE]


def solution(mesh):
    part = P(("blk", "uly"), None)
    return jax.shard_map(
        body,
        mesh=mesh,
        in_specs=(part, part, part, part, P()),
        out_specs=(part, part, part),
        check_vma=False,
    )
```

```python
import functools
import math

import jax
import jax.numpy as jnp
from jax import lax
from jax.experimental import pallas as pl
from jax.experimental.pallas import tpu as pltpu
from jax.sharding import PartitionSpec as P

BLOCK = 128
MAXB = 8
REACH = MAXB - 1
EDGE = 8
MASKED = -1e30
LOG2E = 1.4426950408889634
F32 = jnp.float32
BF16 = jnp.bfloat16
QUERY, DOUT, KEY, VALUE = 0, 1, 2, 3
GKEY, GVALUE, GQUERY = 0, 1, 2


def across(a, b):
    return lax.dot_general(a, b, (((1,), (1,)), ((), ())), preferred_element_type=F32)


def down(a, b):
    return lax.dot_general(a, b, (((0,), (0,)), ((), ())), preferred_element_type=F32)


def plain(a, b):
    return jnp.dot(a, b, preferred_element_type=F32)


def query_pair(n, lead, second, q, d, k, v):
    width = q.shape[-1]
    scale = 1.0 / math.sqrt(width)
    rows = n * BLOCK
    s = across(k, q)
    r = lax.broadcasted_iota(jnp.int32, (rows, 2 * BLOCK), 0)
    c = lax.broadcasted_iota(jnp.int32, (1, 2 * BLOCK), 1)
    low = jnp.where(c < BLOCK, 0, second * BLOCK)
    high = c + (n - 2) * BLOCK
    s = jnp.where((r >= low) & (r <= high), s, MASKED)
    top = jnp.max(s, axis=0, keepdims=True)
    w = jnp.exp2((s - top) * (scale * LOG2E))
    total = jnp.sum(w, axis=0, keepdims=True)
    dp = across(v, d)
    cross = jnp.sum(w * dp, axis=0, keepdims=True)
    inv = 1.0 / total
    delta = cross * inv
    prob = w * inv
    ds = (prob * (dp - delta) * scale).astype(BF16)
    gv = plain(prob.astype(BF16), d)
    gk = plain(ds, q)
    gq = down(ds, k)
    lse = top * (scale * LOG2E) + jnp.log2(total)
    return gq, gk, gv, lse, delta


def inner_kernel(st_ref, x_ref, out_ref, head_ref, tail_ref, near_ref, gk_ref, gv_ref):
    blocks = x_ref.shape[0]
    width = x_ref.shape[-1]
    gk_ref[...] = jnp.zeros_like(gk_ref)
    gv_ref[...] = jnp.zeros_like(gv_ref)
    near_ref[...] = x_ref[:REACH, QUERY : DOUT + 1]

    def tile(t, _):
        first = st_ref[2 * t]
        n_dyn = 2 * t + 2 - first
        second = st_ref[2 * t + 1] - first
        for n in range(2, MAXB + 2):

            @pl.when((first >= 0) & (n_dyn == n))
            def _():
                window = pl.ds(first, n)
                pair = pl.ds(2 * t, 2)
                gq, gk, gv, _, _ = query_pair(
                    n,
                    0,
                    second,
                    x_ref[pair, QUERY].reshape(2 * BLOCK, width),
                    x_ref[pair, DOUT].reshape(2 * BLOCK, width),
                    x_ref[window, KEY].reshape(n * BLOCK, width),
                    x_ref[window, VALUE].reshape(n * BLOCK, width),
                )
                gk_ref[window] += gk.reshape(n, BLOCK, width)
                gv_ref[window] += gv.reshape(n, BLOCK, width)
                out_ref[pair, GQUERY] = gq.astype(BF16).reshape(2, BLOCK, width)

        return 0

    lax.fori_loop(0, blocks // 2, tile, 0)

    def store(i, _):
        out_ref[i, GKEY] = gk_ref[i].astype(BF16)
        out_ref[i, GVALUE] = gv_ref[i].astype(BF16)
        return 0

    lax.fori_loop(0, blocks, store, 0)
    head_ref[:, GKEY] = gk_ref[:EDGE]
    head_ref[:, GVALUE] = gv_ref[:EDGE]
    tail_ref[:, GKEY] = gk_ref[blocks - EDGE :]
    tail_ref[:, GVALUE] = gv_ref[blocks - EDGE :]


def head_kernel(
    st_ref, x_ref, far_ref, head_ref, out_in_ref, out_ref, stat_ref, k_ref, v_ref, gk_ref, gv_ref
):
    width = x_ref.shape[-1]
    k_ref[:REACH] = far_ref[:, 0]
    v_ref[:REACH] = far_ref[:, 1]
    k_ref[REACH:] = x_ref[:, KEY]
    v_ref[REACH:] = x_ref[:, VALUE]
    gk_ref[REACH:] = head_ref[:, GKEY]
    gv_ref[REACH:] = head_ref[:, GVALUE]
    out_ref[:, GQUERY] = out_in_ref[:, GQUERY]
    stat_ref[...] = jnp.full(stat_ref.shape, -MASKED, F32)

    def tile(t, _):
        first = st_ref[2 * t]
        n_dyn = 2 * t + 2 - first
        second = st_ref[2 * t + 1] - first
        for n in range(3, MAXB + 2):

            @pl.when((first < 0) & (n_dyn == n))
            def _():
                window = pl.ds(first + REACH, n)
                pair = pl.ds(2 * t, 2)
                gq, gk, gv, lse, delta = query_pair(
                    n,
                    0,
                    second,
                    x_ref[pair, QUERY].reshape(2 * BLOCK, width),
                    x_ref[pair, DOUT].reshape(2 * BLOCK, width),
                    k_ref[window].reshape(n * BLOCK, width),
                    v_ref[window].reshape(n * BLOCK, width),
                )
                gk_ref[window] += gk.reshape(n, BLOCK, width)
                gv_ref[window] += gv.reshape(n, BLOCK, width)
                out_ref[pair, GQUERY] = gq.astype(BF16).reshape(2, BLOCK, width)
                c = lax.broadcasted_iota(jnp.int32, lse.shape, 1)
                lse = jnp.where((c < BLOCK) | (second == 0), lse, -MASKED)
                stat_ref[t, 0:1, :] = lse
                stat_ref[t, 1:2, :] = delta

        return 0

    lax.fori_loop(0, EDGE // 2, tile, 0)
    out_ref[:, GKEY] = gk_ref[REACH:].astype(BF16)
    out_ref[:, GVALUE] = gv_ref[REACH:].astype(BF16)


def tail_kernel(st_ref, x_ref, near_ref, stat_ref, tail_ref, out_in_ref, out_ref, gk_ref, gv_ref):
    del out_in_ref
    width = x_ref.shape[-1]
    scale = 1.0 / math.sqrt(width)
    gk_ref[...] = tail_ref[:, GKEY]
    gv_ref[...] = tail_ref[:, GVALUE]
    tiles = st_ref[st_ref.shape[0] - 2]
    for t in range(1, EDGE // 2 + 1):

        @pl.when(tiles == t)
        def _():
            many = min(2 * t, REACH)
            rows = many * BLOCK
            q = near_ref[:many, 0].reshape(rows, width)
            d = near_ref[:many, 1].reshape(rows, width)
            lse = jnp.concatenate([stat_ref[i, 0:1, :] for i in range(t)], 1)[:, :rows]
            delta = jnp.concatenate([stat_ref[i, 1:2, :] for i in range(t)], 1)[:, :rows]
            delta = jnp.where(lse < -MASKED, delta, 0.0)

            def key_block(j, _):
                s = across(x_ref[j, KEY], q)
                dp = across(x_ref[j, VALUE], d)
                prob = jnp.exp2(s * (scale * LOG2E) - lse)
                ds = (prob * (dp - delta) * scale).astype(BF16)
                gv_ref[j] += plain(prob.astype(BF16), d)
                gk_ref[j] += plain(ds, q)
                return 0

            lax.fori_loop(st_ref[st_ref.shape[0] - 1], EDGE, key_block, 0)

    out_ref[:, GKEY] = gk_ref[...].astype(BF16)
    out_ref[:, GVALUE] = gv_ref[...].astype(BF16)


def pack_kernel(*refs):
    *arrays, out_ref = refs
    heads, _, _, width = out_ref.shape
    for kind, array in enumerate(arrays):
        for h in range(heads):
            out_ref[h, kind] = array[:, h * width : (h + 1) * width]


def unpack_kernel(back_ref, *refs):
    heads, kinds, _, width = back_ref.shape
    for kind, out in enumerate(refs[len(refs) - kinds :]):
        for h in range(heads):
            out[:, h * width : (h + 1) * width] = back_ref[h, kind]


def whole():
    return pl.BlockSpec(memory_space=pltpu.VMEM)


SMEM = pl.BlockSpec(memory_space=pltpu.SMEM)
PARAMS = pltpu.CompilerParams(vmem_limit_bytes=40 * 1024 * 1024)
WIDE_PARAMS = pltpu.CompilerParams(vmem_limit_bytes=62 * 1024 * 1024)
PACK_PARAMS = pltpu.CompilerParams(vmem_limit_bytes=60 * 1024 * 1024)
STEP = 8


def packed(arrays, half, heads):
    rows, columns = arrays[0].shape
    width = columns // (PHASES * heads)
    steps = heads // STEP
    return pl.pallas_call(
        pack_kernel,
        grid=(steps,),
        out_shape=jax.ShapeDtypeStruct((heads, len(arrays), rows, width), BF16),
        in_specs=[pl.BlockSpec((rows, STEP * width), lambda i: (0, half * steps + i))] * len(arrays),
        out_specs=pl.BlockSpec((STEP, len(arrays), rows, width), lambda i: (i, 0, 0, 0)),
        compiler_params=PACK_PARAMS,
        cost_estimate=pl.CostEstimate(flops=0, bytes_accessed=4 << 20, transcendentals=0),
        name="pack",
    )(*arrays)


def unpacked(back, half, before):
    heads, kinds, rows, width = back.shape
    steps = heads // STEP
    shape = jax.ShapeDtypeStruct((rows, PHASES * heads * width), BF16)
    return pl.pallas_call(
        unpack_kernel,
        grid=(steps,),
        out_shape=(shape,) * kinds,
        in_specs=[pl.BlockSpec((STEP, kinds, rows, width), lambda i: (i, 0, 0, 0))]
        + [pl.BlockSpec(memory_space=pl.ANY)] * len(before),
        out_specs=(pl.BlockSpec((rows, STEP * width), lambda i: (0, half * steps + i)),) * kinds,
        input_output_aliases={1 + i: i for i in range(len(before))},
        compiler_params=PARAMS,
        cost_estimate=pl.CostEstimate(flops=0, bytes_accessed=3 << 20, transcendentals=0),
        name="unpack",
    )(back, *before)


def passed_along(array, by):
    devices = lax.axis_size(("blk", "uly"))
    pairs = [(i, i + by) for i in range(devices) if 0 <= i + by < devices]
    return lax.ppermute(array, ("blk", "uly"), pairs)


def head_grads(starts, x, heads, params):
    blocks = x.shape[0]
    tile_shape = x.shape[2:]
    far = passed_along(x[blocks - REACH :, KEY : VALUE + 1], heads)
    out_type = jax.ShapeDtypeStruct((blocks, 3) + tile_shape, BF16)
    edge_type = jax.ShapeDtypeStruct((EDGE, 2) + tile_shape, F32)
    near_type = jax.ShapeDtypeStruct((REACH, 2) + tile_shape, BF16)
    out, head_acc, tail_acc, near = pl.pallas_call(
        inner_kernel,
        out_shape=(out_type, edge_type, edge_type, near_type),
        in_specs=[SMEM, whole()],
        out_specs=(whole(),) * 4,
        scratch_shapes=[pltpu.VMEM((blocks,) + tile_shape, F32)] * 2,
        compiler_params=params,
        cost_estimate=pl.CostEstimate(flops=8 * 10**9, bytes_accessed=6 << 20, transcendentals=1 << 20),
        name="inner",
    )(starts, x)

    def edge_in(kinds, at):
        return pl.BlockSpec((EDGE, kinds) + tile_shape, lambda i: (at, 0, 0, 0))

    def full(shape):
        return pl.BlockSpec(shape, lambda i: (0,) * len(shape))

    stat_shape = (EDGE // 2, 8, 2 * BLOCK)
    out, stats = pl.pallas_call(
        head_kernel,
        grid=(1,),
        out_shape=(out_type, jax.ShapeDtypeStruct(stat_shape, F32)),
        in_specs=[
            SMEM,
            edge_in(4, 0),
            full((REACH, 2) + tile_shape),
            full((EDGE, 2) + tile_shape),
            edge_in(3, 0),
        ],
        out_specs=(edge_in(3, 0), full(stat_shape)),
        scratch_shapes=[pltpu.VMEM((REACH + EDGE,) + tile_shape, BF16)] * 2
        + [pltpu.VMEM((REACH + EDGE,) + tile_shape, F32)] * 2,
        input_output_aliases={4: 0},
        compiler_params=params,
        cost_estimate=pl.CostEstimate(flops=2 * 10**9, bytes_accessed=3 << 20, transcendentals=1 << 18),
        name="head",
    )(starts, x, far, head_acc, out)
    stats = passed_along(stats, -heads)
    near = passed_along(near, -heads)
    at_end = blocks // EDGE - 1
    return pl.pallas_call(
        tail_kernel,
        grid=(1,),
        out_shape=out_type,
        in_specs=[
            SMEM,
            edge_in(4, at_end),
            full((REACH, 2) + tile_shape),
            full(stat_shape),
            full((EDGE, 2) + tile_shape),
            pl.BlockSpec(memory_space=pl.ANY),
        ],
        out_specs=edge_in(2, at_end),
        scratch_shapes=[pltpu.VMEM((EDGE,) + tile_shape, F32)] * 2,
        input_output_aliases={5: 0},
        compiler_params=params,
        cost_estimate=pl.CostEstimate(flops=2 * 10**9, bytes_accessed=3 << 20, transcendentals=1 << 18),
        name="tail",
    )(starts, x, near, stats, tail_acc, out)


PHASES = 2


def body(queries, keys, values, grad_out, doc_start):
    ulys = lax.axis_size("uly")
    heads = ulys // PHASES
    groups = [list(range(g * heads, (g + 1) * heads)) for g in range(PHASES)]

    blocks = heads * queries.shape[0] // BLOCK
    segment = lax.axis_index("blk") * PHASES + lax.axis_index("uly") // heads
    last = lax.axis_size("blk") * PHASES - 1
    own = lax.dynamic_slice_in_dim(doc_start, segment * blocks, blocks, 0) // BLOCK - segment * blocks
    following = jnp.minimum(segment + 1, last) * blocks
    heads_of = lax.dynamic_slice_in_dim(doc_start, following, EDGE, 0) // BLOCK
    tiles = (jnp.sum(heads_of < following) + 1) // 2
    after = jnp.where(segment == last, EDGE, heads_of[0] - segment * blocks - (blocks - EDGE))
    starts = jnp.concatenate([own, jnp.stack([tiles, after])]).astype(jnp.int32)

    def exchanged(array):
        return lax.all_to_all(
            array, "uly", split_axis=0, concat_axis=0, tiled=True, axis_index_groups=groups
        )

    arrays = (queries, grad_out, keys, values)
    inputs = [exchanged(packed(arrays, p, heads)) for p in range(PHASES)]
    grads = [exchanged(head_grads(starts, x, heads, p)) for x, p in zip(inputs, (WIDE_PARAMS, PARAMS))]
    outs = ()
    for p in range(PHASES):
        outs = unpacked(grads[p], p, outs)
    return outs[GQUERY], outs[GKEY], outs[GVALUE]


def solution(mesh):
    part = P(("blk", "uly"), None)
    return jax.shard_map(
        body,
        mesh=mesh,
        in_specs=(part, part, part, part, P()),
        out_specs=(part, part, part),
        check_vma=False,
    )
```

```python
import functools
import math

import jax
import jax.numpy as jnp
from jax import lax
from jax.experimental import pallas as pl
from jax.experimental.pallas import tpu as pltpu
from jax.sharding import PartitionSpec as P

BLOCK = 128
MAXB = 8
REACH = MAXB - 1
EDGE = 8
MASKED = -1e30
LOG2E = 1.4426950408889634
F32 = jnp.float32
BF16 = jnp.bfloat16
QUERY, DOUT, KEY, VALUE = 0, 1, 2, 3
GKEY, GVALUE, GQUERY = 0, 1, 2


def across(a, b):
    return lax.dot_general(a, b, (((1,), (1,)), ((), ())), preferred_element_type=F32)


def down(a, b):
    return lax.dot_general(a, b, (((0,), (0,)), ((), ())), preferred_element_type=F32)


def plain(a, b):
    return jnp.dot(a, b, preferred_element_type=F32)


def query_pair(n, lead, second, q, d, k, v):
    width = q.shape[-1]
    scale = 1.0 / math.sqrt(width)
    rows = n * BLOCK
    s = across(k, q)
    r = lax.broadcasted_iota(jnp.int32, (rows, 2 * BLOCK), 0)
    c = lax.broadcasted_iota(jnp.int32, (1, 2 * BLOCK), 1)
    low = jnp.where(c < BLOCK, 0, second * BLOCK)
    high = c + (n - 2) * BLOCK
    s = jnp.where((r >= low) & (r <= high), s, MASKED)
    top = jnp.max(s, axis=0, keepdims=True)
    w = jnp.exp2((s - top) * (scale * LOG2E))
    total = jnp.sum(w, axis=0, keepdims=True)
    dp = across(v, d)
    cross = jnp.sum(w * dp, axis=0, keepdims=True)
    inv = 1.0 / total
    delta = cross * inv
    prob = w * inv
    ds = (prob * (dp - delta) * scale).astype(BF16)
    gv = plain(prob.astype(BF16), d)
    gk = plain(ds, q)
    gq = down(ds, k)
    lse = top * (scale * LOG2E) + jnp.log2(total)
    return gq, gk, gv, lse, delta


def inner_kernel(st_ref, x_ref, out_ref, head_ref, tail_ref, near_ref, gk_ref, gv_ref):
    blocks = x_ref.shape[0]
    width = x_ref.shape[-1]
    gk_ref[...] = jnp.zeros_like(gk_ref)
    gv_ref[...] = jnp.zeros_like(gv_ref)
    near_ref[...] = x_ref[:REACH, QUERY : DOUT + 1]

    def tile(t, _):
        first = st_ref[2 * t]
        n_dyn = 2 * t + 2 - first
        second = st_ref[2 * t + 1] - first
        for n in range(2, MAXB + 2):

            @pl.when((first >= 0) & (n_dyn == n))
            def _():
                window = pl.ds(first, n)
                pair = pl.ds(2 * t, 2)
                gq, gk, gv, _, _ = query_pair(
                    n,
                    0,
                    second,
                    x_ref[pair, QUERY].reshape(2 * BLOCK, width),
                    x_ref[pair, DOUT].reshape(2 * BLOCK, width),
                    x_ref[window, KEY].reshape(n * BLOCK, width),
                    x_ref[window, VALUE].reshape(n * BLOCK, width),
                )
                gk_ref[window] += gk.reshape(n, BLOCK, width)
                gv_ref[window] += gv.reshape(n, BLOCK, width)
                out_ref[pair, GQUERY] = gq.astype(BF16).reshape(2, BLOCK, width)

        return 0

    lax.fori_loop(EDGE // 2, blocks // 2, tile, 0)

    def store(i, _):
        out_ref[i, GKEY] = gk_ref[i].astype(BF16)
        out_ref[i, GVALUE] = gv_ref[i].astype(BF16)
        return 0

    lax.fori_loop(EDGE, blocks, store, 0)
    head_ref[:, GKEY] = gk_ref[:EDGE]
    head_ref[:, GVALUE] = gv_ref[:EDGE]
    tail_ref[:, GKEY] = gk_ref[blocks - EDGE :]
    tail_ref[:, GVALUE] = gv_ref[blocks - EDGE :]


def head_kernel(
    st_ref, x_ref, far_ref, head_ref, out_in_ref, out_ref, stat_ref, k_ref, v_ref, gk_ref, gv_ref
):
    del out_in_ref
    width = x_ref.shape[-1]
    k_ref[:REACH] = far_ref[:, 0]
    v_ref[:REACH] = far_ref[:, 1]
    k_ref[REACH:] = x_ref[:, KEY]
    v_ref[REACH:] = x_ref[:, VALUE]
    gk_ref[REACH:] = head_ref[:, GKEY]
    gv_ref[REACH:] = head_ref[:, GVALUE]
    stat_ref[...] = jnp.full(stat_ref.shape, -MASKED, F32)

    def tile(t, _):
        first = st_ref[2 * t]
        n_dyn = 2 * t + 2 - first
        second = st_ref[2 * t + 1] - first
        for n in range(2, MAXB + 2):

            @pl.when(n_dyn == n)
            def _():
                window = pl.ds(first + REACH, n)
                pair = pl.ds(2 * t, 2)
                gq, gk, gv, lse, delta = query_pair(
                    n,
                    0,
                    second,
                    x_ref[pair, QUERY].reshape(2 * BLOCK, width),
                    x_ref[pair, DOUT].reshape(2 * BLOCK, width),
                    k_ref[window].reshape(n * BLOCK, width),
                    v_ref[window].reshape(n * BLOCK, width),
                )
                gk_ref[window] += gk.reshape(n, BLOCK, width)
                gv_ref[window] += gv.reshape(n, BLOCK, width)
                out_ref[pair, GQUERY] = gq.astype(BF16).reshape(2, BLOCK, width)
                c = lax.broadcasted_iota(jnp.int32, lse.shape, 1)
                live = (first < 0) & ((c < BLOCK) | (second == 0))
                lse = jnp.where(live, lse, -MASKED)
                stat_ref[t, 0:1, :] = lse
                stat_ref[t, 1:2, :] = delta

        return 0

    lax.fori_loop(0, EDGE // 2, tile, 0)
    out_ref[:, GKEY] = gk_ref[REACH:].astype(BF16)
    out_ref[:, GVALUE] = gv_ref[REACH:].astype(BF16)


def tail_kernel(st_ref, x_ref, near_ref, stat_ref, tail_ref, out_in_ref, out_ref, gk_ref, gv_ref):
    del out_in_ref
    width = x_ref.shape[-1]
    scale = 1.0 / math.sqrt(width)
    gk_ref[...] = tail_ref[:, GKEY]
    gv_ref[...] = tail_ref[:, GVALUE]
    tiles = st_ref[st_ref.shape[0] - 2]
    for t in range(1, EDGE // 2 + 1):

        @pl.when(tiles == t)
        def _():
            many = min(2 * t, REACH)
            rows = many * BLOCK
            q = near_ref[:many, 0].reshape(rows, width)
            d = near_ref[:many, 1].reshape(rows, width)
            lse = jnp.concatenate([stat_ref[i, 0:1, :] for i in range(t)], 1)[:, :rows]
            delta = jnp.concatenate([stat_ref[i, 1:2, :] for i in range(t)], 1)[:, :rows]
            delta = jnp.where(lse < -MASKED, delta, 0.0)

            def key_block(j, _):
                s = across(x_ref[j, KEY], q)
                dp = across(x_ref[j, VALUE], d)
                prob = jnp.exp2(s * (scale * LOG2E) - lse)
                ds = (prob * (dp - delta) * scale).astype(BF16)
                gv_ref[j] += plain(prob.astype(BF16), d)
                gk_ref[j] += plain(ds, q)
                return 0

            lax.fori_loop(st_ref[st_ref.shape[0] - 1], EDGE, key_block, 0)

    out_ref[:, GKEY] = gk_ref[...].astype(BF16)
    out_ref[:, GVALUE] = gv_ref[...].astype(BF16)


def pack_kernel(*refs):
    *arrays, out_ref = refs
    heads, _, _, width = out_ref.shape
    for kind, array in enumerate(arrays):
        for h in range(heads):
            out_ref[h, kind] = array[:, h * width : (h + 1) * width]


def unpack_kernel(back_ref, *refs):
    heads, kinds, _, width = back_ref.shape
    for kind, out in enumerate(refs[len(refs) - kinds :]):
        for h in range(heads):
            out[:, h * width : (h + 1) * width] = back_ref[h, kind]


def whole():
    return pl.BlockSpec(memory_space=pltpu.VMEM)


SMEM = pl.BlockSpec(memory_space=pltpu.SMEM)
PARAMS = pltpu.CompilerParams(vmem_limit_bytes=40 * 1024 * 1024)
WIDE_PARAMS = pltpu.CompilerParams(vmem_limit_bytes=62 * 1024 * 1024)
PACK_PARAMS = pltpu.CompilerParams(vmem_limit_bytes=60 * 1024 * 1024)
STEP = 8


def packed(arrays, half, heads):
    rows, columns = arrays[0].shape
    width = columns // (PHASES * heads)
    steps = heads // STEP
    return pl.pallas_call(
        pack_kernel,
        grid=(steps,),
        out_shape=jax.ShapeDtypeStruct((heads, len(arrays), rows, width), BF16),
        in_specs=[pl.BlockSpec((rows, STEP * width), lambda i: (0, half * steps + i))] * len(arrays),
        out_specs=pl.BlockSpec((STEP, len(arrays), rows, width), lambda i: (i, 0, 0, 0)),
        compiler_params=PACK_PARAMS,
        cost_estimate=pl.CostEstimate(flops=0, bytes_accessed=4 << 20, transcendentals=0),
        name="pack",
    )(*arrays)


def unpacked(back, half, before):
    heads, kinds, rows, width = back.shape
    steps = heads // STEP
    shape = jax.ShapeDtypeStruct((rows, PHASES * heads * width), BF16)
    return pl.pallas_call(
        unpack_kernel,
        grid=(steps,),
        out_shape=(shape,) * kinds,
        in_specs=[pl.BlockSpec((STEP, kinds, rows, width), lambda i: (i, 0, 0, 0))]
        + [pl.BlockSpec(memory_space=pl.ANY)] * len(before),
        out_specs=(pl.BlockSpec((rows, STEP * width), lambda i: (0, half * steps + i)),) * kinds,
        input_output_aliases={1 + i: i for i in range(len(before))},
        compiler_params=PARAMS,
        cost_estimate=pl.CostEstimate(flops=0, bytes_accessed=3 << 20, transcendentals=0),
        name="unpack",
    )(back, *before)


def passed_along(array, by):
    devices = lax.axis_size(("blk", "uly"))
    pairs = [(i, i + by) for i in range(devices) if 0 <= i + by < devices]
    return lax.ppermute(array, ("blk", "uly"), pairs)


def head_grads(starts, x, heads, params):
    blocks = x.shape[0]
    tile_shape = x.shape[2:]
    far = passed_along(x[blocks - REACH :, KEY : VALUE + 1], heads)
    out_type = jax.ShapeDtypeStruct((blocks, 3) + tile_shape, BF16)
    edge_type = jax.ShapeDtypeStruct((EDGE, 2) + tile_shape, F32)
    near_type = jax.ShapeDtypeStruct((REACH, 2) + tile_shape, BF16)
    out, head_acc, tail_acc, near = pl.pallas_call(
        inner_kernel,
        out_shape=(out_type, edge_type, edge_type, near_type),
        in_specs=[SMEM, whole()],
        out_specs=(whole(),) * 4,
        scratch_shapes=[pltpu.VMEM((blocks,) + tile_shape, F32)] * 2,
        compiler_params=params,
        cost_estimate=pl.CostEstimate(flops=5 * 10**9, bytes_accessed=6 << 20, transcendentals=1 << 20),
        name="inner",
    )(starts, x)

    def edge_in(kinds, at):
        return pl.BlockSpec((EDGE, kinds) + tile_shape, lambda i: (at, 0, 0, 0))

    def full(shape):
        return pl.BlockSpec(shape, lambda i: (0,) * len(shape))

    stat_shape = (EDGE // 2, 8, 2 * BLOCK)
    out, stats = pl.pallas_call(
        head_kernel,
        grid=(1,),
        out_shape=(out_type, jax.ShapeDtypeStruct(stat_shape, F32)),
        in_specs=[
            SMEM,
            edge_in(4, 0),
            full((REACH, 2) + tile_shape),
            full((EDGE, 2) + tile_shape),
            pl.BlockSpec(memory_space=pl.ANY),
        ],
        out_specs=(edge_in(3, 0), full(stat_shape)),
        scratch_shapes=[pltpu.VMEM((REACH + EDGE,) + tile_shape, BF16)] * 2
        + [pltpu.VMEM((REACH + EDGE,) + tile_shape, F32)] * 2,
        input_output_aliases={4: 0},
        compiler_params=params,
        cost_estimate=pl.CostEstimate(flops=5 * 10**9, bytes_accessed=3 << 20, transcendentals=1 << 18),
        name="head",
    )(starts, x, far, head_acc, out)
    stats = passed_along(stats, -heads)
    near = passed_along(near, -heads)
    at_end = blocks // EDGE - 1
    return pl.pallas_call(
        tail_kernel,
        grid=(1,),
        out_shape=out_type,
        in_specs=[
            SMEM,
            edge_in(4, at_end),
            full((REACH, 2) + tile_shape),
            full(stat_shape),
            full((EDGE, 2) + tile_shape),
            pl.BlockSpec(memory_space=pl.ANY),
        ],
        out_specs=edge_in(2, at_end),
        scratch_shapes=[pltpu.VMEM((EDGE,) + tile_shape, F32)] * 2,
        input_output_aliases={5: 0},
        compiler_params=params,
        cost_estimate=pl.CostEstimate(flops=2 * 10**9, bytes_accessed=3 << 20, transcendentals=1 << 18),
        name="tail",
    )(starts, x, near, stats, tail_acc, out)


PHASES = 2


def body(queries, keys, values, grad_out, doc_start):
    ulys = lax.axis_size("uly")
    heads = ulys // PHASES
    groups = [list(range(g * heads, (g + 1) * heads)) for g in range(PHASES)]

    blocks = heads * queries.shape[0] // BLOCK
    segment = lax.axis_index("blk") * PHASES + lax.axis_index("uly") // heads
    last = lax.axis_size("blk") * PHASES - 1
    own = lax.dynamic_slice_in_dim(doc_start, segment * blocks, blocks, 0) // BLOCK - segment * blocks
    following = jnp.minimum(segment + 1, last) * blocks
    heads_of = lax.dynamic_slice_in_dim(doc_start, following, EDGE, 0) // BLOCK
    tiles = (jnp.sum(heads_of < following) + 1) // 2
    after = jnp.where(segment == last, EDGE, heads_of[0] - segment * blocks - (blocks - EDGE))
    starts = jnp.concatenate([own, jnp.stack([tiles, after])]).astype(jnp.int32)

    def exchanged(array):
        return lax.all_to_all(
            array, "uly", split_axis=0, concat_axis=0, tiled=True, axis_index_groups=groups
        )

    arrays = (queries, grad_out, keys, values)
    inputs = [exchanged(packed(arrays, p, heads)) for p in range(PHASES)]
    grads = [exchanged(head_grads(starts, x, heads, p)) for x, p in zip(inputs, (WIDE_PARAMS, PARAMS))]
    outs = ()
    for p in range(PHASES):
        outs = unpacked(grads[p], p, outs)
    return outs[GQUERY], outs[GKEY], outs[GVALUE]


def solution(mesh):
    part = P(("blk", "uly"), None)
    return jax.shard_map(
        body,
        mesh=mesh,
        in_specs=(part, part, part, part, P()),
        out_specs=(part, part, part),
        check_vma=False,
    )
```
